32 devices in a mesh: replica: 4 (over x, core), fsdp: 8 (over z, y).
Axes of the slice: x: 2, y: 2, z: 4, core: 2. Of those that a mesh axis runs over, the one named last changes fastest.
Arguments:
- frag_index: int32 [8], replicated, may hold values from 0 to 7, as said below
- inner_step: int32 [8], replicated, may hold values from 1 to 8, as said below
- inner_params: float32 [4, 8, 65536], P('replica', None, 'fsdp'), may hold values from -6 to 6
- grads: bfloat16 [4, 8, 65536], P('replica', None, 'fsdp'), may hold values from -6 to 6
- adam_first: float32 [4, 8, 65536], P('replica', None, 'fsdp'), may hold values from -4 to 4
- adam_second: float32 [4, 8, 65536], P('replica', None, 'fsdp'), may hold values from 0.01 to 1
- outer_params: float32 [8, 65536], P(None, 'fsdp'), may hold values from -6 to 6
- outer_momentum: float32 [8, 65536], P(None, 'fsdp'), may hold values from -6 to 6
Outputs:
- new_inner: float32 [4, 8, 65536], P('replica', None, 'fsdp')
- new_first: float32 [4, 8, 65536], P('replica', None, 'fsdp')
- new_second: float32 [4, 8, 65536], P('replica', None, 'fsdp')
- new_outer: float32 [8, 65536], P(None, 'fsdp')
- new_momentum: float32 [8, 65536], P(None, 'fsdp')
- refreshed: bfloat16 [65536], replicated
The draws below stay inside these ranges and needn't reach their ends.
Inputs may be any that keep to these rules, and one draw needn't show every extreme that they name: `frag_index`: each fragment number exactly once. `inner_step`: each count of 1 to 8 exactly once.
All inputs are finite; a program needn't handle non-finite values.
Results may differ from the reference program's by a relative error of at most 0.00075.
Values may be sent and summed in bfloat16 or wider, within the bound.
No kernel may reach another device: no remote copies, remote signals or barrier semaphores. Data moves between devices by JAX's collectives and lax.ppermute only.
A program may use at most 64 MiB of HBM per device.

```python
import math
import jax
import jax.numpy as jnp
from jax import lax

FRAGS = 8
FRAG = 65536
REPLICAS = 4
N_REPLICA = 4


def draw_frag_index(key, part):
    folded = jax.random.fold_in(key, 7301)
    return jax.random.permutation(folded, FRAGS).astype(jnp.int32)


def draw_inner_step(key, part):
    folded = jax.random.fold_in(key, 9203)
    return (1 + jax.random.permutation(folded, FRAGS)).astype(jnp.int32)


def shard_levels(stream_key, dims, pieces, smallest, high):
    gain, own = 1.0, jax.random.fold_in(stream_key, 6)
    for axis_at, parts in pieces:
        steps = jnp.exp(jax.random.uniform(jax.random.fold_in(own, axis_at), (parts,), jnp.float32, smallest / len(pieces), high / len(pieces)))
        gain = gain * jnp.repeat(steps, dims[axis_at] // parts).reshape([-1 if axis == axis_at else 1 for axis in range(len(dims))])
    return gain


def scatter_about(own_key, extent, deviation, most, pieces=(), held_as=jnp.bfloat16):
    level = shard_levels(own_key, extent, pieces, -0.22, 0.18) if pieces else 1.0
    result = jax.random.normal(own_key, extent, jnp.float32) * deviation * level
    return jnp.minimum(jnp.maximum(result, -most), most).astype(held_as)


def setup_inputs(seed: int = 0) -> dict:
    streams_of = jax.random.split(jax.random.key(seed), 9)
    frag_index = draw_frag_index(jax.random.fold_in(streams_of[8], 71), 0)
    inner_step = draw_inner_step(jax.random.fold_in(streams_of[8], 71), 0)
    inner_params = scatter_about(streams_of[2], (REPLICAS, FRAGS, FRAG), 1.0, 6.0, ((0, 4), (2, 8)), jnp.float32)
    grads = scatter_about(streams_of[3], (REPLICAS, FRAGS, FRAG), 1.0, 6.0, ((0, 4), (2, 8)))
    adam_first = scatter_about(streams_of[4], (REPLICAS, FRAGS, FRAG), 0.3, 4.0, ((0, 4), (2, 8)), jnp.float32)
    adam_second = jnp.clip(jnp.exp(math.log(1.0) - 4.6051702 * jax.random.uniform(streams_of[5], (REPLICAS, FRAGS, FRAG), jnp.float32) ** shard_levels(streams_of[5], (REPLICAS, FRAGS, FRAG), ((0, 4), (2, 8)), -0.2, 0.2)), 0.01, 1.0)
    outer_params = scatter_about(streams_of[6], (FRAGS, FRAG), 1.0, 6.0, ((1, 8),), jnp.float32)
    outer_momentum = scatter_about(streams_of[7], (FRAGS, FRAG), 0.5, 6.0, ((1, 8),), jnp.float32)
    return dict(frag_index=frag_index, inner_step=inner_step, inner_params=inner_params, grads=grads, adam_first=adam_first, adam_second=adam_second, outer_params=outer_params, outer_momentum=outer_momentum)


beta_first = 0.9
beta_second = 0.95
adam_eps = 1e-08
inner_rate = 0.05
decay_rate = 0.1
outer_rate = 0.7
momentum_keep = 0.9
mix_local = 0.5

def reference(frag_index, inner_step, inner_params, grads, adam_first, adam_second, outer_params, outer_momentum):
    fragment = frag_index[0]
    step_count = inner_step.astype(jnp.float32)[None, :, None]
    grad_wide = grads.astype(jnp.float32)
    first_moment = beta_first * adam_first + (1.0 - beta_first) * grad_wide
    second_moment = beta_second * adam_second + (1.0 - beta_second) * grad_wide * grad_wide
    first_fix = 1.0 - jnp.power(jnp.float32(beta_first), step_count)
    second_fix = 1.0 - jnp.power(jnp.float32(beta_second), step_count)
    stepped = inner_params * (1.0 - inner_rate * decay_rate) - inner_rate * (first_moment / first_fix) / (jnp.sqrt(second_moment / second_fix) + adam_eps)
    inner_row = lax.dynamic_index_in_dim(inner_params, fragment, 1, keepdims=False)
    outer_row = lax.dynamic_index_in_dim(outer_params, fragment, 0, keepdims=False)
    moment_row = lax.dynamic_index_in_dim(outer_momentum, fragment, 0, keepdims=False)
    mean_drift = lax.optimization_barrier(jnp.sum(outer_row[None, :] - inner_row, axis=0)) / N_REPLICA
    new_moment_row = momentum_keep * moment_row + mean_drift
    new_outer_row = outer_row - outer_rate * (mean_drift + momentum_keep * new_moment_row)
    refreshed = new_outer_row.astype(jnp.bfloat16)
    stepped_row = lax.dynamic_index_in_dim(stepped, fragment, 1, keepdims=False)
    blended = mix_local * stepped_row + (1.0 - mix_local) * refreshed.astype(jnp.float32)[None, :]
    new_inner = lax.dynamic_update_index_in_dim(stepped, blended, fragment, 1)
    new_outer = lax.dynamic_update_index_in_dim(outer_params, new_outer_row, fragment, 0)
    new_momentum = lax.dynamic_update_index_in_dim(outer_momentum, new_moment_row, fragment, 0)
    return (new_inner, first_moment, second_moment, new_outer, new_momentum, refreshed)
```

```python
import jax
import jax.numpy as jnp
from jax import lax
from jax.sharding import PartitionSpec as P

beta_first = 0.9
beta_second = 0.95
adam_eps = 1e-08
inner_rate = 0.05
decay_rate = 0.1
outer_rate = 0.7
momentum_keep = 0.9
mix_local = 0.5

AXES = ("replica", "fsdp")
LANES = 128


def nesterov(outer_row, moment_row, mean_drift):
    new_moment_row = momentum_keep * moment_row + mean_drift
    new_outer_row = outer_row - outer_rate * (mean_drift + momentum_keep * new_moment_row)
    return (new_outer_row, new_moment_row)


def swap(block, replica_bits, fsdp_bits):
    replicas, shards = lax.axis_size("replica"), lax.axis_size("fsdp")
    pairs = [
        (r * shards + s, (r ^ replica_bits) * shards + (s ^ fsdp_bits))
        for r in range(replicas)
        for s in range(shards)
    ]
    return lax.ppermute(block, AXES, pairs)


def sum_over_replicas(block):
    bit = 1
    while bit < lax.axis_size("replica"):
        block = block + swap(block, bit | 1, 0)
        bit *= 2
    return block


def gather_over_fsdp(block):
    shard = lax.axis_index("fsdp")
    held = block[None]
    bit = 1
    while bit < lax.axis_size("fsdp"):
        other = swap(held, 1, bit)
        upper = (shard & bit) != 0
        held = jnp.concatenate([jnp.where(upper, other, held), jnp.where(upper, held, other)])
        bit *= 2
    return held


def on_device(
    frag_index,
    inner_step,
    inner_params,
    grads,
    adam_first,
    adam_second,
    outer_params,
    outer_momentum,
):
    fragment = frag_index[0]
    replicas = lax.axis_size("replica")
    width = inner_params.shape[2]
    tile = (width // LANES, LANES)

    def row_of(table):
        return lax.dynamic_index_in_dim(table, fragment, 0, keepdims=False).reshape(tile)

    inner_row = row_of(inner_params[0])
    outer_row = row_of(outer_params)
    moment_row = row_of(outer_momentum)
    summed = sum_over_replicas(outer_row - inner_row)
    new_outer_row, new_moment_row = nesterov(outer_row, moment_row, summed / replicas)
    refreshed_shard = new_outer_row.astype(jnp.bfloat16)
    refreshed = gather_over_fsdp(refreshed_shard).reshape(-1)
    step_count = inner_step.astype(jnp.float32)[None, :, None]
    grad_wide = grads.astype(jnp.float32)
    first_moment = beta_first * adam_first + (1.0 - beta_first) * grad_wide
    second_moment = beta_second * adam_second + (1.0 - beta_second) * grad_wide * grad_wide
    first_fix = 1.0 - jnp.power(jnp.float32(beta_first), step_count)
    second_fix = 1.0 - jnp.power(jnp.float32(beta_second), step_count)
    stepped = inner_params * (1.0 - inner_rate * decay_rate) - inner_rate * (
        first_moment / first_fix
    ) / (jnp.sqrt(second_moment / second_fix) + adam_eps)
    stepped_row = lax.dynamic_index_in_dim(stepped, fragment, 1, keepdims=False)
    blended = mix_local * stepped_row + (1.0 - mix_local) * refreshed_shard.astype(
        jnp.float32
    ).reshape(1, width)
    new_inner = lax.dynamic_update_index_in_dim(stepped, blended, fragment, 1)
    new_outer = lax.dynamic_update_index_in_dim(
        outer_params, new_outer_row.reshape(width), fragment, 0
    )
    new_momentum = lax.dynamic_update_index_in_dim(
        outer_momentum, new_moment_row.reshape(width), fragment, 0
    )
    return (new_inner, first_moment, second_moment, new_outer, new_momentum, refreshed)


def solution(mesh):
    return jax.shard_map(
        on_device,
        mesh=mesh,
        in_specs=(
            P(),
            P(),
            P("replica", None, "fsdp"),
            P("replica", None, "fsdp"),
            P("replica", None, "fsdp"),
            P("replica", None, "fsdp"),
            P(None, "fsdp"),
            P(None, "fsdp"),
        ),
        out_specs=(
            P("replica", None, "fsdp"),
            P("replica", None, "fsdp"),
            P("replica", None, "fsdp"),
            P(None, "fsdp"),
            P(None, "fsdp"),
            P(),
        ),
        check_vma=False,
    )
```

```python
import jax
import jax.numpy as jnp
from jax import lax
from jax.experimental import pallas as pl
from jax.experimental.pallas import tpu as pltpu
from jax.sharding import PartitionSpec as P

beta_first = 0.9
beta_second = 0.95
adam_eps = 1e-08
inner_rate = 0.05
decay_rate = 0.1
outer_rate = 0.7
momentum_keep = 0.9
mix_local = 0.5

AXES = ("replica", "fsdp")
LANES = 128
SUBLANES = 8


def nesterov(outer_row, moment_row, mean_drift):
    new_moment_row = momentum_keep * moment_row + mean_drift
    new_outer_row = outer_row - outer_rate * (mean_drift + momentum_keep * new_moment_row)
    return (new_outer_row, new_moment_row)


def begin_kernel(
    index_hbm, inner_hbm, outer_hbm, moment_hbm, drift, outer, moment, index, inner, sems
):
    sources = (index_hbm, inner_hbm.at[0], outer_hbm, moment_hbm)
    targets = (index, inner, outer, moment)
    copies = [
        pltpu.make_async_copy(source, target, sems.at[i])
        for i, (source, target) in enumerate(zip(sources, targets))
    ]
    for copy in copies:
        copy.start()
    for copy in copies[:3]:
        copy.wait()
    fragment = index[0]
    sublane = lax.broadcasted_iota(jnp.int32, (SUBLANES, LANES), 0)
    for top in range(0, drift.shape[0], SUBLANES):
        folded = jnp.zeros((SUBLANES, LANES), jnp.float32)
        for i in range(SUBLANES):
            columns = pl.ds((top + i) * LANES, LANES)
            every = outer[:, columns] - inner[:, columns]
            turned = pltpu.roll(every, (i + SUBLANES - fragment) % SUBLANES, 0)
            folded = jnp.where(sublane == i, turned, folded)
        drift[pl.ds(top, SUBLANES), :] = folded
    copies[3].wait()


def begin(frag_index, inner_params, outer_params, outer_momentum):
    frags, width = outer_params.shape
    return pl.pallas_call(
        begin_kernel,
        out_shape=(
            pltpu.VMEM((width // LANES, LANES), jnp.float32),
            pltpu.VMEM((frags, width), jnp.float32),
            pltpu.VMEM((frags, width), jnp.float32),
        ),
        in_specs=[pl.BlockSpec(memory_space=pl.ANY)] * 4,
        out_specs=[pl.BlockSpec(memory_space=pltpu.VMEM)] * 3,
        scratch_shapes=[
            pltpu.SMEM(frag_index.shape, jnp.int32),
            pltpu.VMEM((frags, width), jnp.float32),
            pltpu.SemaphoreType.DMA((4,)),
        ],
        name="begin",
    )(frag_index, inner_params, outer_params, outer_momentum)


def swap(block, replica_bits, fsdp_bits):
    replicas, shards = lax.axis_size("replica"), lax.axis_size("fsdp")
    pairs = [
        (r * shards + s, (r ^ replica_bits) * shards + (s ^ fsdp_bits))
        for r in range(replicas)
        for s in range(shards)
    ]
    return lax.ppermute(block, AXES, pairs)


def after(arrays, earlier):
    return lax.optimization_barrier((tuple(arrays), earlier))[0]


def gather_upper(block):
    shard = lax.axis_index("fsdp")
    held = block[None]
    bit = lax.axis_size("fsdp") // 2
    while bit > 2:
        other = swap(held, 1, bit)
        upper = (shard & bit) != 0
        held = jnp.stack(
            [jnp.where(upper, other, held), jnp.where(upper, held, other)], axis=1
        ).reshape(-1, *block.shape)
        bit //= 2
    return held


def gather_lower(held):
    shard = lax.axis_index("fsdp")
    first, second, both = (swap(held, 1, bits) for bits in (1, 2, 3))
    even, odd, low = (shard & 1) == 0, (shard & 1) != 0, (shard & 2) == 0
    near = (jnp.where(even, held, first), jnp.where(even, first, held))
    far = (jnp.where(odd, both, second), jnp.where(odd, second, both))
    lower = [jnp.where(low, n, f) for n, f in zip(near, far)]
    upper = [jnp.where(low, f, n) for n, f in zip(near, far)]
    return jnp.stack(lower + upper, axis=1)


def on_device(
    frag_index,
    inner_step,
    inner_params,
    grads,
    adam_first,
    adam_second,
    outer_params,
    outer_momentum,
):
    fragment = frag_index[0]
    replicas = lax.axis_size("replica")
    frags, width = outer_params.shape
    chosen = (jnp.arange(frags) == fragment)[:, None]

    def row_of(table):
        row = lax.dynamic_index_in_dim(table, fragment, 0, keepdims=False)
        return row.reshape(width // LANES, LANES)

    def put_row(row, table):
        return jnp.where(chosen, row.reshape(1, width), table)

    drift, outer_params, outer_momentum = begin(
        frag_index, inner_params, outer_params, outer_momentum
    )
    summed = drift + swap(drift, 1, 0)
    inner_params, grads, adam_first, adam_second = after(
        (inner_params, grads, adam_first, adam_second), summed
    )
    bit = 2
    while bit < replicas:
        summed = summed + swap(summed, bit | 1, 0)
        bit *= 2

    step_count = inner_step.astype(jnp.float32)[None, :, None]
    grad_wide = grads.astype(jnp.float32)
    first_moment = beta_first * adam_first + (1.0 - beta_first) * grad_wide
    second_moment = beta_second * adam_second + (1.0 - beta_second) * grad_wide * grad_wide
    first_fix = 1.0 - jnp.power(jnp.float32(beta_first), step_count)
    second_fix = 1.0 - jnp.power(jnp.float32(beta_second), step_count)
    stepped = inner_params * (1.0 - inner_rate * decay_rate) - inner_rate * (
        first_moment / first_fix
    ) / (jnp.sqrt(second_moment / second_fix) + adam_eps)

    outer_row, moment_row = row_of(outer_params), row_of(outer_momentum)
    new_outer_row, new_moment_row = nesterov(outer_row, moment_row, summed / replicas)
    refreshed_shard = new_outer_row.astype(jnp.bfloat16)
    held = gather_upper(refreshed_shard)
    new_outer = put_row(new_outer_row, outer_params)
    new_momentum = put_row(new_moment_row, outer_momentum)
    refreshed = gather_lower(held).reshape(-1)
    stepped, refreshed_shard = after((stepped, refreshed_shard), held)
    refreshed_row = refreshed_shard.astype(jnp.float32).reshape(1, 1, width)
    blended = mix_local * stepped + (1.0 - mix_local) * refreshed_row
    new_inner = jnp.where(chosen[None], blended, stepped)
    return (new_inner, first_moment, second_moment, new_outer, new_momentum, refreshed)


def solution(mesh):
    return jax.shard_map(
        on_device,
        mesh=mesh,
        in_specs=(
            P(),
            P(),
            P("replica", None, "fsdp"),
            P("replica", None, "fsdp"),
            P("replica", None, "fsdp"),
            P("replica", None, "fsdp"),
            P(None, "fsdp"),
            P(None, "fsdp"),
        ),
        out_specs=(
            P("replica", None, "fsdp"),
            P("replica", None, "fsdp"),
            P("replica", None, "fsdp"),
            P(None, "fsdp"),
            P(None, "fsdp"),
            P(),
        ),
        check_vma=False,
    )
```

```python
import jax
import jax.numpy as jnp
from jax import lax
from jax.experimental import pallas as pl
from jax.experimental.pallas import tpu as pltpu
from jax.sharding import PartitionSpec as P

beta_first = 0.9
beta_second = 0.95
adam_eps = 1e-08
inner_rate = 0.05
decay_rate = 0.1
outer_rate = 0.7
momentum_keep = 0.9
mix_local = 0.5

AXES = ("replica", "fsdp")
LANES = 128
SUBLANES = 8


def nesterov(outer_row, moment_row, mean_drift):
    new_moment_row = momentum_keep * moment_row + mean_drift
    new_outer_row = outer_row - outer_rate * (mean_drift + momentum_keep * new_moment_row)
    return (new_outer_row, new_moment_row)


def begin_kernel(*refs):
    sources, targets, sems = refs[:4], refs[4:8], refs[8]
    copies = [
        pltpu.make_async_copy(source, target, sems.at[i])
        for i, (source, target) in enumerate(zip(sources, targets))
    ]
    for copy in copies:
        copy.start()
    for copy in copies:
        copy.wait()


def begin(*arrays):
    memories = (pltpu.SMEM,) + (pltpu.VMEM,) * 3
    return pl.pallas_call(
        begin_kernel,
        out_shape=[memory(x.shape, x.dtype) for memory, x in zip(memories, arrays)],
        in_specs=[pl.BlockSpec(memory_space=pl.ANY)] * 4,
        out_specs=[pl.BlockSpec(memory_space=memory) for memory in memories],
        scratch_shapes=[pltpu.SemaphoreType.DMA((4,))],
        name="begin",
    )(*arrays)


def fold(columns, fragment, folded):
    sublane = lax.broadcasted_iota(jnp.int32, (SUBLANES, LANES), 0)
    turns = [(i + SUBLANES - fragment) % SUBLANES for i in range(SUBLANES)]
    for top in range(0, folded.shape[0], SUBLANES):
        tile = jnp.zeros((SUBLANES, LANES), jnp.float32)
        for i in range(SUBLANES):
            turned = pltpu.roll(columns(pl.ds((top + i) * LANES, LANES)), turns[i], 0)
            tile = jnp.where(sublane == i, turned, tile)
        folded[pl.ds(top, SUBLANES), :] = tile


def drift_kernel(index, outer, inner, other, drift):
    def both(at):
        return (outer[:, at] - inner[0, :, at]) + (outer[:, at] - other[:, at])

    fold(both, index[0], drift)


def rows_kernel(index, outer, moment, outer_row, moment_row, chosen):
    fold(lambda at: outer[:, at], index[0], outer_row)
    fold(lambda at: moment[:, at], index[0], moment_row)
    sublane = lax.broadcasted_iota(jnp.int32, chosen.shape, 0)
    chosen[...] = (sublane == index[0]).astype(jnp.int32)


def in_fast_memory(kernel, index, tables, shapes):
    memory = pltpu.VMEM
    return pl.pallas_call(
        kernel,
        out_shape=[memory(shape, dtype) for shape, dtype in shapes],
        in_specs=[pl.BlockSpec(memory_space=pltpu.SMEM)]
        + [pl.BlockSpec(memory_space=memory)] * len(tables),
        out_specs=[pl.BlockSpec(memory_space=memory)] * len(shapes),
        name=kernel.__name__,
    )(index, *(pltpu.with_memory_space_constraint(table, memory) for table in tables))


def swap(block, replica_bits, fsdp_bits):
    replicas, shards = lax.axis_size("replica"), lax.axis_size("fsdp")
    pairs = [
        (r * shards + s, (r ^ replica_bits) * shards + (s ^ fsdp_bits))
        for r in range(replicas)
        for s in range(shards)
    ]
    return lax.ppermute(block, AXES, pairs)


def after(arrays, earlier):
    return lax.optimization_barrier((tuple(arrays), earlier))[0]


def gather_upper(block):
    shard = lax.axis_index("fsdp")
    held = block[None]
    bit = lax.axis_size("fsdp") // 2
    while bit > 2:
        other = swap(held, 1, bit)
        upper = (shard & bit) != 0
        held = jnp.stack(
            [jnp.where(upper, other, held), jnp.where(upper, held, other)], axis=1
        ).reshape(-1, *block.shape)
        bit //= 2
    return held


def gather_lower(held):
    shard = lax.axis_index("fsdp")
    first, second, both = (swap(held, 1, bits) for bits in (1, 2, 3))
    even, odd, low = (shard & 1) == 0, (shard & 1) != 0, (shard & 2) == 0
    near = (jnp.where(even, held, first), jnp.where(even, first, held))
    far = (jnp.where(odd, both, second), jnp.where(odd, second, both))
    lower = [jnp.where(low, n, f) for n, f in zip(near, far)]
    upper = [jnp.where(low, f, n) for n, f in zip(near, far)]
    return jnp.stack(lower + upper, axis=1)


def on_device(
    frag_index,
    inner_step,
    inner_params,
    grads,
    adam_first,
    adam_second,
    outer_params,
    outer_momentum,
):
    replicas = lax.axis_size("replica")
    frags, width = outer_params.shape
    other_inner = swap(inner_params[0], 1, 0)
    index, inner_params, outer_params, outer_momentum = begin(
        frag_index, inner_params, outer_params, outer_momentum
    )
    row = ((width // LANES, LANES), jnp.float32)
    (summed,) = in_fast_memory(
        drift_kernel, index, (outer_params, inner_params, other_inner), (row,)
    )
    (inner_params,) = after((inner_params,), summed)
    bit = 2
    while bit < replicas:
        summed = summed + swap(summed, bit | 1, 0)
        bit *= 2

    step_count = inner_step.astype(jnp.float32)[None, :, None]
    grad_wide = grads.astype(jnp.float32)
    first_moment = beta_first * adam_first + (1.0 - beta_first) * grad_wide
    second_moment = beta_second * adam_second + (1.0 - beta_second) * grad_wide * grad_wide
    first_fix = 1.0 - jnp.power(jnp.float32(beta_first), step_count)
    second_fix = 1.0 - jnp.power(jnp.float32(beta_second), step_count)
    stepped = inner_params * (1.0 - inner_rate * decay_rate) - inner_rate * (
        first_moment / first_fix
    ) / (jnp.sqrt(second_moment / second_fix) + adam_eps)

    outer_params, outer_momentum = after((outer_params, outer_momentum), stepped)
    outer_row, moment_row, chosen = in_fast_memory(
        rows_kernel, index, (outer_params, outer_momentum), (row, row, ((frags, LANES), jnp.int32))
    )
    chosen = chosen[:, :1] != 0

    def put_row(row, table):
        return jnp.where(chosen, row.reshape(1, width), table)

    new_outer_row, new_moment_row = nesterov(outer_row, moment_row, summed / replicas)
    refreshed_shard = new_outer_row.astype(jnp.bfloat16)
    held = gather_upper(refreshed_shard)
    new_outer = put_row(new_outer_row, outer_params)
    new_momentum = put_row(new_moment_row, outer_momentum)
    refreshed = gather_lower(held).reshape(-1)
    stepped, refreshed_shard = after((stepped, refreshed_shard), held)
    refreshed_row = refreshed_shard.astype(jnp.float32).reshape(1, 1, width)
    blended = mix_local * stepped + (1.0 - mix_local) * refreshed_row
    new_inner = jnp.where(chosen[None], blended, stepped)
    return (new_inner, first_moment, second_moment, new_outer, new_momentum, refreshed)


def solution(mesh):
    return jax.shard_map(
        on_device,
        mesh=mesh,
        in_specs=(
            P(),
            P(),
            P("replica", None, "fsdp"),
            P("replica", None, "fsdp"),
            P("replica", None, "fsdp"),
            P("replica", None, "fsdp"),
            P(None, "fsdp"),
            P(None, "fsdp"),
        ),
        out_specs=(
            P("replica", None, "fsdp"),
            P("replica", None, "fsdp"),
            P("replica", None, "fsdp"),
            P(None, "fsdp"),
            P(None, "fsdp"),
            P(),
        ),
        check_vma=False,
    )
```

```python
import jax
import jax.numpy as jnp
from jax import lax
from jax.experimental import pallas as pl
from jax.experimental.pallas import tpu as pltpu
from jax.sharding import PartitionSpec as P

beta_first = 0.9
beta_second = 0.95
adam_eps = 1e-08
inner_rate = 0.05
decay_rate = 0.1
outer_rate = 0.7
momentum_keep = 0.9
mix_local = 0.5

AXES = ("replica", "fsdp")
LANES = 128
SUBLANES = 8


def begin_kernel(*refs):
    sources, targets, sems = refs[:4], refs[4:8], refs[8]
    copies = [
        pltpu.make_async_copy(source, target, sems.at[i])
        for i, (source, target) in enumerate(zip(sources, targets))
    ]
    for copy in copies:
        copy.start()
    for copy in copies:
        copy.wait()


def begin(*arrays):
    memories = (pltpu.SMEM,) + (pltpu.VMEM,) * 3
    return pl.pallas_call(
        begin_kernel,
        out_shape=[memory(x.shape, x.dtype) for memory, x in zip(memories, arrays)],
        in_specs=[pl.BlockSpec(memory_space=pl.ANY)] * 4,
        out_specs=[pl.BlockSpec(memory_space=memory) for memory in memories],
        scratch_shapes=[pltpu.SemaphoreType.DMA((4,))],
        name="begin",
    )(*arrays)


def fold(columns, fragment, folded):
    sublane = lax.broadcasted_iota(jnp.int32, (SUBLANES, LANES), 0)
    turns = [(i + SUBLANES - fragment) % SUBLANES for i in range(SUBLANES)]
    for top in range(0, folded.shape[0], SUBLANES):
        tile = jnp.zeros((SUBLANES, LANES), jnp.float32)
        for i in range(SUBLANES):
            turned = pltpu.roll(columns(pl.ds((top + i) * LANES, LANES)), turns[i], 0)
            tile = jnp.where(sublane == i, turned, tile)
        folded[pl.ds(top, SUBLANES), :] = tile


def rows_kernel(index, outer, inner, other, moment, drift, share, moment_row, chosen):
    def drifts(at):
        return (outer[:, at] - inner[0, :, at]) + (outer[:, at] - other[:, at])

    fold(drifts, index[0], drift)
    fold(lambda at: moment[:, at], index[0], moment_row)
    fold(lambda at: outer[:, at], index[0], share)
    share[...] = 0.5 * (share[...] - outer_rate * momentum_keep * momentum_keep * moment_row[...])
    sublane = lax.broadcasted_iota(jnp.int32, chosen.shape, 0)
    chosen[...] = (sublane == index[0]).astype(jnp.int32)


def in_fast_memory(kernel, index, tables, shapes):
    memory = pltpu.VMEM
    return pl.pallas_call(
        kernel,
        out_shape=[memory(shape, dtype) for shape, dtype in shapes],
        in_specs=[pl.BlockSpec(memory_space=pltpu.SMEM)]
        + [pl.BlockSpec(memory_space=memory)] * len(tables),
        out_specs=[pl.BlockSpec(memory_space=memory)] * len(shapes),
        name=kernel.__name__,
    )(index, *(pltpu.with_memory_space_constraint(table, memory) for table in tables))


def swap(block, replica_bits, fsdp_bits):
    replicas, shards = lax.axis_size("replica"), lax.axis_size("fsdp")
    pairs = [
        (r * shards + s, (r ^ replica_bits) * shards + (s ^ fsdp_bits))
        for r in range(replicas)
        for s in range(shards)
    ]
    return lax.ppermute(block, AXES, pairs)


def after(arrays, earlier):
    return lax.optimization_barrier((tuple(arrays), earlier))[0]


def bit_of(axis, bit):
    return (lax.axis_index(axis) & bit) != 0


def ring(near, far, replica_bit, fsdp_bits):
    fsdp_a, fsdp_b = fsdp_bits
    replicas, shards = lax.axis_size("replica"), lax.axis_size("fsdp")
    pairs = []
    for r in range(replicas):
        for s in range(shards):
            a = (r & replica_bit) != 0 or (s & fsdp_a) != 0
            across = s ^ fsdp_a if (r & 1) == a else s ^ fsdp_a ^ fsdp_b
            pairs.append((r * shards + s, (r ^ replica_bit ^ 1) * shards + across))
    got = lax.ppermute(far, AXES, pairs)
    across_b = swap(near, 1, fsdp_b)
    other = swap(got, 1, 0)
    got, other, across_b = lax.optimization_barrier((got, other, across_b))
    a = bit_of("replica", replica_bit) | bit_of("fsdp", fsdp_a)
    is_a = bit_of("replica", 1) == a
    return jnp.where(is_a, got, other), across_b, jnp.where(is_a, other, got)


def in_order(bit, own, other):
    return jnp.where(bit, other, own), jnp.where(bit, own, other)


def on_device(
    frag_index,
    inner_step,
    inner_params,
    grads,
    adam_first,
    adam_second,
    outer_params,
    outer_momentum,
):
    replicas = lax.axis_size("replica")
    frags, width = outer_params.shape
    other_inner = swap(inner_params[0], 1, 0)
    index, inner_params, outer_params, outer_momentum = begin(
        frag_index, inner_params, outer_params, outer_momentum
    )
    row = ((width // LANES, LANES), jnp.float32)
    drift, share, moment_row, chosen = in_fast_memory(
        rows_kernel,
        index,
        (outer_params, inner_params, other_inner, outer_momentum),
        (row, row, row, ((frags, LANES), jnp.int32)),
    )
    chosen = chosen[:, :1] != 0

    def put_row(row, table):
        return jnp.where(chosen, row.reshape(1, width), table)

    half = replicas // 2
    bit = 2
    while bit < half:
        drift = drift + swap(drift, bit | 1, 0)
        bit *= 2

    def part(drift):
        return share - (outer_rate * (1.0 + momentum_keep) / replicas) * drift

    same_row = bit_of("replica", 1) == bit_of("replica", half)
    far = jnp.where(same_row, drift, part(drift))
    drift_across, near_across, far_across = ring(part(drift), far, half, (0, 2))

    inner_params, outer_params, outer_momentum = after(
        (inner_params, outer_params, outer_momentum), far
    )
    step_count = inner_step.astype(jnp.float32)[None, :, None]
    grad_wide = grads.astype(jnp.float32)
    first_moment = beta_first * adam_first + (1.0 - beta_first) * grad_wide
    second_moment = beta_second * adam_second + (1.0 - beta_second) * grad_wide * grad_wide
    first_fix = 1.0 - jnp.power(jnp.float32(beta_first), step_count)
    second_fix = 1.0 - jnp.power(jnp.float32(beta_second), step_count)
    stepped = inner_params * (1.0 - inner_rate * decay_rate) - inner_rate * (
        first_moment / first_fix
    ) / (jnp.sqrt(second_moment / second_fix) + adam_eps)

    mean_drift = (drift + drift_across) / replicas
    new_moment_row = momentum_keep * moment_row + mean_drift
    new_outer_row = part(drift) + part(drift_across)
    refreshed_shard = new_outer_row.astype(jnp.bfloat16)
    next_shard = (near_across + far_across).astype(jnp.bfloat16)
    held = jnp.stack(in_order(bit_of("fsdp", 2), refreshed_shard, next_shard))
    bit = 8
    while bit < lax.axis_size("fsdp"):
        held = jnp.stack(in_order(bit_of("fsdp", bit), held, swap(held, 1, bit)))
        bit *= 2
    across_4, across_1, across_5 = ring(held, held, 0, (4, 1))
    odd = bit_of("fsdp", 1)
    own_4 = jnp.stack(in_order(odd, held, across_1), axis=-3)
    other_4 = jnp.stack(in_order(odd, across_4, across_5), axis=-3)
    refreshed = jnp.stack(in_order(bit_of("fsdp", 4), own_4, other_4), axis=-5).reshape(-1)

    stepped, refreshed_shard, outer_params, outer_momentum = after(
        (stepped, refreshed_shard, outer_params, outer_momentum), held
    )
    new_outer = put_row(new_outer_row, outer_params)
    new_momentum = put_row(new_moment_row, outer_momentum)
    refreshed_row = refreshed_shard.astype(jnp.float32).reshape(1, 1, width)
    blended = mix_local * stepped + (1.0 - mix_local) * refreshed_row
    new_inner = jnp.where(chosen[None], blended, stepped)
    return (new_inner, first_moment, second_moment, new_outer, new_momentum, refreshed)


def solution(mesh):
    return jax.shard_map(
        on_device,
        mesh=mesh,
        in_specs=(
            P(),
            P(),
            P("replica", None, "fsdp"),
            P("replica", None, "fsdp"),
            P("replica", None, "fsdp"),
            P("replica", None, "fsdp"),
            P(None, "fsdp"),
            P(None, "fsdp"),
        ),
        out_specs=(
            P("replica", None, "fsdp"),
            P("replica", None, "fsdp"),
            P("replica", None, "fsdp"),
            P(None, "fsdp"),
            P(None, "fsdp"),
            P(),
        ),
        check_vma=False,
    )
```

```python
import jax
import jax.numpy as jnp
from jax import lax
from jax.experimental import pallas as pl
from jax.experimental.pallas import tpu as pltpu
from jax.sharding import PartitionSpec as P

beta_first = 0.9
beta_second = 0.95
adam_eps = 1e-08
inner_rate = 0.05
decay_rate = 0.1
outer_rate = 0.7
momentum_keep = 0.9
mix_local = 0.5

AXES = ("replica", "fsdp")
LANES = 128
SUBLANES = 8


def begin_kernel(*refs):
    sources, targets, sems = refs[:4], refs[4:8], refs[8]
    copies = [
        pltpu.make_async_copy(source, target, sems.at[i])
        for i, (source, target) in enumerate(zip(sources, targets))
    ]
    for copy in copies:
        copy.start()
    for copy in copies:
        copy.wait()


def begin(*arrays):
    memories = (pltpu.SMEM,) + (pltpu.VMEM,) * 3
    return pl.pallas_call(
        begin_kernel,
        out_shape=[memory(x.shape, x.dtype) for memory, x in zip(memories, arrays)],
        in_specs=[pl.BlockSpec(memory_space=pl.ANY)] * 4,
        out_specs=[pl.BlockSpec(memory_space=memory) for memory in memories],
        scratch_shapes=[pltpu.SemaphoreType.DMA((4,))],
        name="begin",
    )(*arrays)


def fold(columns, fragment, folded):
    sublane = lax.broadcasted_iota(jnp.int32, (SUBLANES, LANES), 0)
    turns = [(i + SUBLANES - fragment) % SUBLANES for i in range(SUBLANES)]
    for top in range(0, folded.shape[0], SUBLANES):
        tile = jnp.zeros((SUBLANES, LANES), jnp.float32)
        for i in range(SUBLANES):
            turned = pltpu.roll(columns(pl.ds((top + i) * LANES, LANES)), turns[i], 0)
            tile = jnp.where(sublane == i, turned, tile)
        folded[pl.ds(top, SUBLANES), :] = tile


def rows_kernel(index, outer, inner, other, moment, drift, share, moment_row, chosen):
    def drifts(at):
        return (outer[:, at] - inner[0, :, at]) + (outer[:, at] - other[:, at])

    fold(drifts, index[0], drift)
    fold(lambda at: moment[:, at], index[0], moment_row)
    fold(lambda at: outer[:, at], index[0], share)
    share[...] = 0.5 * (share[...] - outer_rate * momentum_keep * momentum_keep * moment_row[...])
    sublane = lax.broadcasted_iota(jnp.int32, chosen.shape, 0)
    chosen[...] = (sublane == index[0]).astype(jnp.int32)


def in_fast_memory(kernel, index, tables, shapes):
    memory = pltpu.VMEM
    return pl.pallas_call(
        kernel,
        out_shape=[memory(shape, dtype) for shape, dtype in shapes],
        in_specs=[pl.BlockSpec(memory_space=pltpu.SMEM)]
        + [pl.BlockSpec(memory_space=memory)] * len(tables),
        out_specs=[pl.BlockSpec(memory_space=memory)] * len(shapes),
        name=kernel.__name__,
    )(index, *(pltpu.with_memory_space_constraint(table, memory) for table in tables))


def swap(block, replica_bits, fsdp_bits):
    replicas, shards = lax.axis_size("replica"), lax.axis_size("fsdp")
    pairs = [
        (r * shards + s, (r ^ replica_bits) * shards + (s ^ fsdp_bits))
        for r in range(replicas)
        for s in range(shards)
    ]
    return lax.ppermute(block, AXES, pairs)


def after(arrays, earlier):
    return lax.optimization_barrier((tuple(arrays), earlier))[0]


def bit_of(axis, bit):
    return (lax.axis_index(axis) & bit) != 0


def ring(near, far, replica_bit, fsdp_bits):
    fsdp_a, fsdp_b = fsdp_bits
    replicas, shards = lax.axis_size("replica"), lax.axis_size("fsdp")
    pairs = []
    for r in range(replicas):
        for s in range(shards):
            a = (r & replica_bit) != 0 or (s & fsdp_a) != 0
            across = s ^ fsdp_a if (r & 1) == a else s ^ fsdp_a ^ fsdp_b
            pairs.append((r * shards + s, (r ^ replica_bit ^ 1) * shards + across))
    got = lax.ppermute(far, AXES, pairs)
    across_b = swap(near, 1, fsdp_b)
    other = swap(got, 1, 0)
    got, other, across_b = lax.optimization_barrier((got, other, across_b))
    a = bit_of("replica", replica_bit) | bit_of("fsdp", fsdp_a)
    is_a = bit_of("replica", 1) == a
    return got, other, across_b, is_a


def in_order(bit, own, other):
    return jnp.where(bit, other, own), jnp.where(bit, own, other)


def order_kernel(own, across_1, got, other, refreshed, sems):
    core = lax.axis_index("replica") % 2
    four, one = (lax.axis_index("fsdp") // 4) % 2, lax.axis_index("fsdp") % 2
    straight = (core + four + 1) % 2
    far = ((one + 1 + straight) % 2, (one + straight) % 2)
    blocks, rows = own.shape[0], own.shape[1]
    copies = []
    for source, at_4, at_1 in (
        (own, four, one),
        (across_1, four, 1 - one),
        (got, 1 - four, far[0]),
        (other, 1 - four, far[1]),
    ):
        for i in range(blocks):
            place = ((i // 2 * 2 + at_4) * 2 + i % 2) * 2 + at_1
            target = refreshed.at[pl.ds(pl.multiple_of(place * rows, rows), rows), :]
            copies.append(pltpu.make_async_copy(source.at[i], target, sems.at[len(copies)]))
    for copy in copies:
        copy.start()
    for copy in copies:
        copy.wait()


def put_in_order(*sources):
    rows, lanes = sources[0].shape[-2:]
    sources = [x.reshape(-1, rows, lanes) for x in sources]
    count = 4 * sources[0].shape[0]
    return pl.pallas_call(
        order_kernel,
        out_shape=jax.ShapeDtypeStruct((count * rows, lanes), sources[0].dtype),
        in_specs=[pl.BlockSpec(memory_space=pltpu.VMEM)] * 4,
        out_specs=pl.BlockSpec(memory_space=pltpu.HBM),
        scratch_shapes=[pltpu.SemaphoreType.DMA((count,))],
        name="order",
    )(*(pltpu.with_memory_space_constraint(x, pltpu.VMEM) for x in sources)).reshape(-1)


def on_device(
    frag_index,
    inner_step,
    inner_params,
    grads,
    adam_first,
    adam_second,
    outer_params,
    outer_momentum,
):
    replicas = lax.axis_size("replica")
    frags, width = outer_params.shape
    other_inner = swap(inner_params[0], 1, 0)
    index, inner_params, outer_params, outer_momentum = begin(
        frag_index, inner_params, outer_params, outer_momentum
    )
    row = ((width // LANES, LANES), jnp.float32)
    drift, share, moment_row, chosen = in_fast_memory(
        rows_kernel,
        index,
        (outer_params, inner_params, other_inner, outer_momentum),
        (row, row, row, ((frags, LANES), jnp.int32)),
    )
    chosen = chosen[:, :1] != 0

    def put_row(row, table):
        return jnp.where(chosen, row.reshape(1, width), table)

    half = replicas // 2
    bit = 2
    while bit < half:
        drift = drift + swap(drift, bit | 1, 0)
        bit *= 2

    def part(drift):
        return share - (outer_rate * (1.0 + momentum_keep) / replicas) * drift

    same_row = bit_of("replica", 1) == bit_of("replica", half)
    far = jnp.where(same_row, drift, part(drift))
    got, other, near_across, is_a = ring(part(drift), far, half, (0, 2))
    drift_across, far_across = jnp.where(is_a, got, other), jnp.where(is_a, other, got)

    inner_params, outer_params, outer_momentum = after(
        (inner_params, outer_params, outer_momentum), far
    )
    step_count = inner_step.astype(jnp.float32)[None, :, None]
    grad_wide = grads.astype(jnp.float32)
    first_moment = beta_first * adam_first + (1.0 - beta_first) * grad_wide
    second_moment = beta_second * adam_second + (1.0 - beta_second) * grad_wide * grad_wide
    first_fix = 1.0 - jnp.power(jnp.float32(beta_first), step_count)
    second_fix = 1.0 - jnp.power(jnp.float32(beta_second), step_count)
    stepped = inner_params * (1.0 - inner_rate * decay_rate) - inner_rate * (
        first_moment / first_fix
    ) / (jnp.sqrt(second_moment / second_fix) + adam_eps)

    mean_drift = (drift + drift_across) / replicas
    new_moment_row = momentum_keep * moment_row + mean_drift
    new_outer_row = part(drift) + part(drift_across)
    refreshed_shard = new_outer_row.astype(jnp.bfloat16)
    next_shard = (near_across + far_across).astype(jnp.bfloat16)
    held = jnp.stack(in_order(bit_of("fsdp", 2), refreshed_shard, next_shard))
    bit = 8
    while bit < lax.axis_size("fsdp"):
        held = jnp.stack(in_order(bit_of("fsdp", bit), held, swap(held, 1, bit)))
        bit *= 2
    got, other, across_1, _ = ring(held, held, 0, (4, 1))
    refreshed = put_in_order(held, across_1, got, other)

    stepped, refreshed_shard, outer_params, outer_momentum = after(
        (stepped, refreshed_shard, outer_params, outer_momentum), held
    )
    new_outer = put_row(new_outer_row, outer_params)
    new_momentum = put_row(new_moment_row, outer_momentum)
    refreshed_row = refreshed_shard.astype(jnp.float32).reshape(1, 1, width)
    blended = mix_local * stepped + (1.0 - mix_local) * refreshed_row
    new_inner = jnp.where(chosen[None], blended, stepped)
    return (new_inner, first_moment, second_moment, new_outer, new_momentum, refreshed)


def solution(mesh):
    return jax.shard_map(
        on_device,
        mesh=mesh,
        in_specs=(
            P(),
            P(),
            P("replica", None, "fsdp"),
            P("replica", None, "fsdp"),
            P("replica", None, "fsdp"),
            P("replica", None, "fsdp"),
            P(None, "fsdp"),
            P(None, "fsdp"),
        ),
        out_specs=(
            P("replica", None, "fsdp"),
            P("replica", None, "fsdp"),
            P("replica", None, "fsdp"),
            P(None, "fsdp"),
            P(None, "fsdp"),
            P(),
        ),
        check_vma=False,
    )
```

```python
import jax
import jax.numpy as jnp
from jax import lax
from jax.experimental import pallas as pl
from jax.experimental.pallas import tpu as pltpu
from jax.sharding import PartitionSpec as P

beta_first = 0.9
beta_second = 0.95
adam_eps = 1e-08
inner_rate = 0.05
decay_rate = 0.1
outer_rate = 0.7
momentum_keep = 0.9
mix_local = 0.5

AXES = ("replica", "fsdp")
LANES = 128
SUBLANES = 8


def begin_kernel(*refs):
    sources, targets, sems = refs[:4], refs[4:8], refs[8]
    copies = [
        pltpu.make_async_copy(source, target, sems.at[i])
        for i, (source, target) in enumerate(zip(sources, targets))
    ]
    for copy in copies:
        copy.start()
    for copy in copies:
        copy.wait()


def begin(*arrays):
    memories = (pltpu.SMEM,) + (pltpu.VMEM,) * 3
    return pl.pallas_call(
        begin_kernel,
        out_shape=[memory(x.shape, x.dtype) for memory, x in zip(memories, arrays)],
        in_specs=[pl.BlockSpec(memory_space=pl.ANY)] * 4,
        out_specs=[pl.BlockSpec(memory_space=memory) for memory in memories],
        scratch_shapes=[pltpu.SemaphoreType.DMA((4,))],
        name="begin",
    )(*arrays)


def fold(columns, fragment, folded):
    sublane = lax.broadcasted_iota(jnp.int32, (SUBLANES, LANES), 0)
    turns = [(i + SUBLANES - fragment) % SUBLANES for i in range(SUBLANES)]
    for top in range(0, folded.shape[0], SUBLANES):
        tile = jnp.zeros((SUBLANES, LANES), jnp.float32)
        for i in range(SUBLANES):
            turned = pltpu.roll(columns(pl.ds((top + i) * LANES, LANES)), turns[i], 0)
            tile = jnp.where(sublane == i, turned, tile)
        folded[pl.ds(top, SUBLANES), :] = tile


def rows_kernel(index, outer, inner, other, moment, drift, share, moment_row, chosen):
    def drifts(at):
        return (outer[:, at] - inner[0, :, at]) + (outer[:, at] - other[:, at])

    fold(drifts, index[0], drift)
    fold(lambda at: moment[:, at], index[0], moment_row)
    fold(lambda at: outer[:, at], index[0], share)
    share[...] = 0.5 * (share[...] - outer_rate * momentum_keep * momentum_keep * moment_row[...])
    sublane = lax.broadcasted_iota(jnp.int32, chosen.shape, 0)
    chosen[...] = (sublane == index[0]).astype(jnp.int32)


def in_fast_memory(kernel, index, tables, shapes):
    memory = pltpu.VMEM
    return pl.pallas_call(
        kernel,
        out_shape=[memory(shape, dtype) for shape, dtype in shapes],
        in_specs=[pl.BlockSpec(memory_space=pltpu.SMEM)]
        + [pl.BlockSpec(memory_space=memory)] * len(tables),
        out_specs=[pl.BlockSpec(memory_space=memory)] * len(shapes),
        name=kernel.__name__,
    )(index, *(pltpu.with_memory_space_constraint(table, memory) for table in tables))


def swap(block, replica_bits, fsdp_bits):
    replicas, shards = lax.axis_size("replica"), lax.axis_size("fsdp")
    pairs = [
        (r * shards + s, (r ^ replica_bits) * shards + (s ^ fsdp_bits))
        for r in range(replicas)
        for s in range(shards)
    ]
    return lax.ppermute(block, AXES, pairs)


def after(arrays, earlier):
    return lax.optimization_barrier((tuple(arrays), earlier))[0]


def bit_of(axis, bit):
    return (lax.axis_index(axis) & bit) != 0


def ring(near, far, replica_bit, fsdp_bits):
    fsdp_a, fsdp_b = fsdp_bits
    replicas, shards = lax.axis_size("replica"), lax.axis_size("fsdp")
    pairs = []
    for r in range(replicas):
        for s in range(shards):
            a = (r & replica_bit) != 0 or (s & fsdp_a) != 0
            across = s ^ fsdp_a if (r & 1) == a else s ^ fsdp_a ^ fsdp_b
            pairs.append((r * shards + s, (r ^ replica_bit ^ 1) * shards + across))
    got = lax.ppermute(far, AXES, pairs)
    across_b = swap(near, 1, fsdp_b)
    other = swap(got, 1, 0)
    got, other, across_b = lax.optimization_barrier((got, other, across_b))
    a = bit_of("replica", replica_bit) | bit_of("fsdp", fsdp_a)
    is_a = bit_of("replica", 1) == a
    return got, other, across_b, is_a


def in_order(bit, own, other):
    return jnp.where(bit, other, own), jnp.where(bit, own, other)


def order_kernel(own, across_1, got, other, refreshed, sems):
    core = lax.axis_index("replica") % 2
    shard = lax.axis_index("fsdp")
    four, two, one = (shard // 4) % 2, (shard // 2) % 2, shard % 2
    straight = (core + four + 1) % 2
    far = ((one + 1 + straight) % 2, (one + straight) % 2)
    blocks, rows = own.shape[0], own.shape[1]
    copies = []
    for source, at_4, at_1 in (
        (own, four, one),
        (across_1, four, 1 - one),
        (got, 1 - four, far[0]),
        (other, 1 - four, far[1]),
    ):
        for i in range(blocks):
            place = ((i // 2 * 2 + at_4) * 2 + (i + two) % 2) * 2 + at_1
            target = refreshed.at[pl.ds(pl.multiple_of(place * rows, rows), rows), :]
            copies.append(pltpu.make_async_copy(source.at[i], target, sems.at[len(copies)]))
    for copy in copies:
        copy.start()
    for copy in copies:
        copy.wait()


def put_in_order(*sources):
    rows, lanes = sources[0].shape[-2:]
    sources = [x.reshape(-1, rows, lanes) for x in sources]
    count = 4 * sources[0].shape[0]
    return pl.pallas_call(
        order_kernel,
        out_shape=jax.ShapeDtypeStruct((count * rows, lanes), sources[0].dtype),
        in_specs=[pl.BlockSpec(memory_space=pltpu.VMEM)] * 4,
        out_specs=pl.BlockSpec(memory_space=pltpu.HBM),
        scratch_shapes=[pltpu.SemaphoreType.DMA((count,))],
        name="order",
    )(*(pltpu.with_memory_space_constraint(x, pltpu.VMEM) for x in sources)).reshape(-1)


def on_device(
    frag_index,
    inner_step,
    inner_params,
    grads,
    adam_first,
    adam_second,
    outer_params,
    outer_momentum,
):
    replicas = lax.axis_size("replica")
    frags, width = outer_params.shape
    other_inner = swap(inner_params[0], 1, 0)
    index, inner_params, outer_params, outer_momentum = begin(
        frag_index, inner_params, outer_params, outer_momentum
    )
    row = ((width // LANES, LANES), jnp.float32)
    drift, share, moment_row, chosen = in_fast_memory(
        rows_kernel,
        index,
        (outer_params, inner_params, other_inner, outer_momentum),
        (row, row, row, ((frags, LANES), jnp.int32)),
    )
    chosen = chosen[:, :1] != 0

    def put_row(row, table):
        return jnp.where(chosen, row.reshape(1, width), table)

    half = replicas // 2
    bit = 2
    while bit < half:
        drift = drift + swap(drift, bit | 1, 0)
        bit *= 2

    def part(drift):
        return share - (outer_rate * (1.0 + momentum_keep) / replicas) * drift

    same_row = bit_of("replica", 1) == bit_of("replica", half)
    far = jnp.where(same_row, drift, part(drift))
    got, other, near_across, is_a = ring(part(drift), far, half, (0, 2))
    drift_across, far_across = jnp.where(is_a, got, other), jnp.where(is_a, other, got)

    inner_params, outer_params, outer_momentum = after(
        (inner_params, outer_params, outer_momentum), far
    )
    step_count = inner_step.astype(jnp.float32)[None, :, None]
    grad_wide = grads.astype(jnp.float32)
    first_moment = beta_first * adam_first + (1.0 - beta_first) * grad_wide
    second_moment = beta_second * adam_second + (1.0 - beta_second) * grad_wide * grad_wide
    first_fix = 1.0 - jnp.power(jnp.float32(beta_first), step_count)
    second_fix = 1.0 - jnp.power(jnp.float32(beta_second), step_count)
    stepped = inner_params * (1.0 - inner_rate * decay_rate) - inner_rate * (
        first_moment / first_fix
    ) / (jnp.sqrt(second_moment / second_fix) + adam_eps)

    mean_drift = (drift + drift_across) / replicas
    new_moment_row = momentum_keep * moment_row + mean_drift
    new_outer_row = part(drift) + part(drift_across)
    refreshed_shard = new_outer_row.astype(jnp.bfloat16)
    next_shard = (near_across + far_across).astype(jnp.bfloat16)
    held = jnp.stack((refreshed_shard, next_shard))
    bit = 8
    while bit < lax.axis_size("fsdp"):
        held = jnp.stack(in_order(bit_of("fsdp", bit), held, swap(held, 1, bit)))
        bit *= 2
    got, other, across_1, _ = ring(held, held, 0, (4, 1))
    refreshed = put_in_order(held, across_1, got, other)

    stepped, refreshed_shard, outer_params, outer_momentum = after(
        (stepped, refreshed_shard, outer_params, outer_momentum), held
    )
    new_outer = put_row(new_outer_row, outer_params)
    new_momentum = put_row(new_moment_row, outer_momentum)
    refreshed_row = refreshed_shard.astype(jnp.float32).reshape(1, 1, width)
    blended = mix_local * stepped + (1.0 - mix_local) * refreshed_row
    new_inner = jnp.where(chosen[None], blended, stepped)
    return (new_inner, first_moment, second_moment, new_outer, new_momentum, refreshed)


def solution(mesh):
    return jax.shard_map(
        on_device,
        mesh=mesh,
        in_specs=(
            P(),
            P(),
            P("replica", None, "fsdp"),
            P("replica", None, "fsdp"),
            P("replica", None, "fsdp"),
            P("replica", None, "fsdp"),
            P(None, "fsdp"),
            P(None, "fsdp"),
        ),
        out_specs=(
            P("replica", None, "fsdp"),
            P("replica", None, "fsdp"),
            P("replica", None, "fsdp"),
            P(None, "fsdp"),
            P(None, "fsdp"),
            P(),
        ),
        check_vma=False,
    )
```

```python
import jax
import jax.numpy as jnp
from jax import lax
from jax.experimental import pallas as pl
from jax.experimental.pallas import tpu as pltpu
from jax.sharding import PartitionSpec as P

beta_first = 0.9
beta_second = 0.95
adam_eps = 1e-08
inner_rate = 0.05
decay_rate = 0.1
outer_rate = 0.7
momentum_keep = 0.9
mix_local = 0.5

AXES = ("replica", "fsdp")
LANES = 128
SUBLANES = 8


def begin_kernel(*refs):
    sources, targets, sems = refs[:5], refs[5:10], refs[10]
    copies = [
        pltpu.make_async_copy(source, target, sems.at[i])
        for i, (source, target) in enumerate(zip(sources, targets))
    ]
    for copy in copies:
        copy.start()
    for copy in copies:
        copy.wait()


def begin(*arrays):
    memories = (pltpu.SMEM,) + (pltpu.VMEM,) * 4
    return pl.pallas_call(
        begin_kernel,
        out_shape=[memory(x.shape, x.dtype) for memory, x in zip(memories, arrays)],
        in_specs=[pl.BlockSpec(memory_space=pl.ANY)] * 5,
        out_specs=[pl.BlockSpec(memory_space=memory) for memory in memories],
        scratch_shapes=[pltpu.SemaphoreType.DMA((5,))],
        name="begin",
    )(*arrays)


def fold(columns, fragment, folded):
    sublane = lax.broadcasted_iota(jnp.int32, (SUBLANES, LANES), 0)
    turns = [(i + SUBLANES - fragment) % SUBLANES for i in range(SUBLANES)]
    for top in range(0, folded.shape[0], SUBLANES):
        tile = jnp.zeros((SUBLANES, LANES), jnp.float32)
        for i in range(SUBLANES):
            turned = pltpu.roll(columns(pl.ds((top + i) * LANES, LANES)), turns[i], 0)
            tile = jnp.where(sublane == i, turned, tile)
        folded[pl.ds(top, SUBLANES), :] = tile


def rows_kernel(index, outer, moment, share, moment_row, chosen):
    fold(lambda at: moment[:, at], index[0], moment_row)
    fold(lambda at: outer[:, at], index[0], share)
    share[...] = 0.5 * (share[...] - outer_rate * momentum_keep * momentum_keep * moment_row[...])
    sublane = lax.broadcasted_iota(jnp.int32, chosen.shape, 0)
    chosen[...] = (sublane == index[0]).astype(jnp.int32)


def drift_kernel(index, outer, inner, other, drift):
    def drifts(at):
        return (outer[:, at] - inner[0, :, at]) + (outer[:, at] - other[:, at])

    fold(drifts, index[0], drift)


def in_fast_memory(kernel, index, tables, shapes):
    memory = pltpu.VMEM
    return pl.pallas_call(
        kernel,
        out_shape=[memory(shape, dtype) for shape, dtype in shapes],
        in_specs=[pl.BlockSpec(memory_space=pltpu.SMEM)]
        + [pl.BlockSpec(memory_space=memory)] * len(tables),
        out_specs=[pl.BlockSpec(memory_space=memory)] * len(shapes),
        name=kernel.__name__,
    )(index, *(pltpu.with_memory_space_constraint(table, memory) for table in tables))


def swap(block, replica_bits, fsdp_bits):
    replicas, shards = lax.axis_size("replica"), lax.axis_size("fsdp")
    pairs = [
        (r * shards + s, (r ^ replica_bits) * shards + (s ^ fsdp_bits))
        for r in range(replicas)
        for s in range(shards)
    ]
    return lax.ppermute(block, AXES, pairs)


def after(arrays, earlier):
    return lax.optimization_barrier((tuple(arrays), earlier))[0]


def bit_of(axis, bit):
    return (lax.axis_index(axis) & bit) != 0


def ring(near, far, replica_bit, fsdp_bits):
    fsdp_a, fsdp_b = fsdp_bits
    replicas, shards = lax.axis_size("replica"), lax.axis_size("fsdp")
    pairs = []
    for r in range(replicas):
        for s in range(shards):
            a = (r & replica_bit) != 0 or (s & fsdp_a) != 0
            across = s ^ fsdp_a if (r & 1) == a else s ^ fsdp_a ^ fsdp_b
            pairs.append((r * shards + s, (r ^ replica_bit ^ 1) * shards + across))
    got = lax.ppermute(far, AXES, pairs)
    across_b = swap(near, 1, fsdp_b)
    other = swap(got, 1, 0)
    got, other, across_b = lax.optimization_barrier((got, other, across_b))
    a = bit_of("replica", replica_bit) | bit_of("fsdp", fsdp_a)
    is_a = bit_of("replica", 1) == a
    return got, other, across_b, is_a


def in_order(bit, own, other):
    return jnp.where(bit, other, own), jnp.where(bit, own, other)


def order_kernel(own, across_1, got, other, refreshed, sems):
    core = lax.axis_index("replica") % 2
    shard = lax.axis_index("fsdp")
    four, two, one = (shard // 4) % 2, (shard // 2) % 2, shard % 2
    straight = (core + four + 1) % 2
    far = ((one + 1 + straight) % 2, (one + straight) % 2)
    blocks, rows = own.shape[0], own.shape[1]
    copies = []
    for source, at_4, at_1 in (
        (own, four, one),
        (across_1, four, 1 - one),
        (got, 1 - four, far[0]),
        (other, 1 - four, far[1]),
    ):
        for i in range(blocks):
            place = ((i // 2 * 2 + at_4) * 2 + (i + two) % 2) * 2 + at_1
            target = refreshed.at[pl.ds(pl.multiple_of(place * rows, rows), rows), :]
            copies.append(pltpu.make_async_copy(source.at[i], target, sems.at[len(copies)]))
    for copy in copies:
        copy.start()
    for copy in copies:
        copy.wait()


def put_in_order(*sources):
    rows, lanes = sources[0].shape[-2:]
    sources = [x.reshape(-1, rows, lanes) for x in sources]
    count = 4 * sources[0].shape[0]
    return pl.pallas_call(
        order_kernel,
        out_shape=jax.ShapeDtypeStruct((count * rows, lanes), sources[0].dtype),
        in_specs=[pl.BlockSpec(memory_space=pltpu.VMEM)] * 4,
        out_specs=pl.BlockSpec(memory_space=pltpu.HBM),
        scratch_shapes=[pltpu.SemaphoreType.DMA((count,))],
        name="order",
    )(*(pltpu.with_memory_space_constraint(x, pltpu.VMEM) for x in sources)).reshape(-1)


def on_device(
    frag_index,
    inner_step,
    inner_params,
    grads,
    adam_first,
    adam_second,
    outer_params,
    outer_momentum,
):
    replicas = lax.axis_size("replica")
    frags, width = outer_params.shape
    other_inner = swap(inner_params[0], 1, 0)
    index, inner_params, outer_params, outer_momentum, inner_step = begin(
        frag_index, inner_params, outer_params, outer_momentum, inner_step
    )
    row = ((width // LANES, LANES), jnp.float32)
    share, moment_row, chosen = in_fast_memory(
        rows_kernel,
        index,
        (outer_params, outer_momentum),
        (row, row, ((frags, LANES), jnp.int32)),
    )
    (drift,) = in_fast_memory(
        drift_kernel, index, (outer_params, inner_params, other_inner), (row,)
    )
    half = replicas // 2
    bit = 2
    while bit < half:
        drift = drift + swap(drift, bit | 1, 0)
        bit *= 2

    def part(drift):
        return share - (outer_rate * (1.0 + momentum_keep) / replicas) * drift

    same_row = bit_of("replica", 1) == bit_of("replica", half)
    far = jnp.where(same_row, drift, part(drift))
    got, other, near_across, is_a = ring(part(drift), far, half, (0, 2))
    drift_across, far_across = jnp.where(is_a, got, other), jnp.where(is_a, other, got)

    inner_params, inner_step = after((inner_params, inner_step), far)
    step_count = inner_step.astype(jnp.float32)[None, :, None]
    grad_wide = grads.astype(jnp.float32)
    first_moment = beta_first * adam_first + (1.0 - beta_first) * grad_wide
    second_moment = beta_second * adam_second + (1.0 - beta_second) * grad_wide * grad_wide
    first_fix = 1.0 - jnp.power(jnp.float32(beta_first), step_count)
    second_fix = 1.0 - jnp.power(jnp.float32(beta_second), step_count)
    stepped = inner_params * (1.0 - inner_rate * decay_rate) - inner_rate * (
        first_moment / first_fix
    ) / (jnp.sqrt(second_moment / second_fix) + adam_eps)

    mean_drift = (drift + drift_across) / replicas
    new_moment_row = momentum_keep * moment_row + mean_drift
    new_outer_row = part(drift) + part(drift_across)
    refreshed_shard = new_outer_row.astype(jnp.bfloat16)
    next_shard = (near_across + far_across).astype(jnp.bfloat16)
    held = jnp.stack((refreshed_shard, next_shard))
    bit = 8
    while bit < lax.axis_size("fsdp"):
        held = jnp.stack(in_order(bit_of("fsdp", bit), held, swap(held, 1, bit)))
        bit *= 2
    got, other, across_1, _ = ring(held, held, 0, (4, 1))
    refreshed = put_in_order(held, across_1, got, other)

    stepped, refreshed_shard, chosen, outer_params, outer_momentum = after(
        (stepped, refreshed_shard, chosen, outer_params, outer_momentum), held
    )
    chosen = chosen[:, :1] != 0

    def put_row(row, table):
        return jnp.where(chosen, row.reshape(1, width), table)

    new_outer = put_row(new_outer_row, outer_params)
    new_momentum = put_row(new_moment_row, outer_momentum)
    refreshed_row = refreshed_shard.astype(jnp.float32).reshape(1, 1, width)
    blended = mix_local * stepped + (1.0 - mix_local) * refreshed_row
    new_inner = jnp.where(chosen[None], blended, stepped)
    return (new_inner, first_moment, second_moment, new_outer, new_momentum, refreshed)


def solution(mesh):
    return jax.shard_map(
        on_device,
        mesh=mesh,
        in_specs=(
            P(),
            P(),
            P("replica", None, "fsdp"),
            P("replica", None, "fsdp"),
            P("replica", None, "fsdp"),
            P("replica", None, "fsdp"),
            P(None, "fsdp"),
            P(None, "fsdp"),
        ),
        out_specs=(
            P("replica", None, "fsdp"),
            P("replica", None, "fsdp"),
            P("replica", None, "fsdp"),
            P(None, "fsdp"),
            P(None, "fsdp"),
            P(),
        ),
        check_vma=False,
    )
```
